32 devices in a mesh: groups: 2 (over y), attn: 4 (over z), expert: 4 (over x, core).
Axes of the slice: x: 2, y: 2, z: 4, core: 2. Of those that a mesh axis runs over, the one named last changes fastest.
Arguments:
- hidden_in: bfloat16 [512, 6144], P(('groups', 'attn')), parts along dimension 0, may hold values from -6 to 6
- queries: bfloat16 [512, 6144], P(('groups', 'attn'), 'expert'), parts along dimension 0, may hold values from -5 to 5
- keys: bfloat16 [512, 1024], P(('groups', 'attn'), 'expert'), parts along dimension 0, may hold values from -5 to 5
- values: bfloat16 [512, 1024], P(('groups', 'attn'), 'expert'), parts along dimension 0, may hold values from -6 to 6
- norm_gain: bfloat16 [6144], replicated, may hold values from 0.099609375 to 1.8984375
- routes: int32 [512, 2], P(('groups', 'attn')), parts along dimension 0, may hold values from 0 to 3, all different within a row; in each aligned block of 64 rows (0 to 63, 64 to 127, ...) at most 48 rows name the same one
- gate_codes: int32 [512, 2], P(('groups', 'attn')), parts along dimension 0, may hold values from 1 to 255
- lengths: int32 [8], P('groups'), parts along dimension 0, may hold values from 1 to 128, 256 in all
- w_gate: bfloat16 [4, 6144, 8192], P('expert', None, 'attn'), may hold values from -0.078125 to 0.078125
- w_up: bfloat16 [4, 6144, 8192], P('expert', None, 'attn'), may hold values from -0.078125 to 0.078125
- w_down: bfloat16 [4, 8192, 6144], P('expert', 'attn'), may hold values from -0.0625 to 0.0625
Outputs:
- mixed: bfloat16 [512, 6144], P(('groups', 'attn'), 'expert'), parts along dimension 0
The draws below stay inside these ranges and needn't reach their ends.
There are 2 independent parts, one for each index of `groups`. The reference program is written for one: setup_inputs(seed, part) draws one part's arguments, and reference() takes and returns one part's arrays. A program takes and returns all parts, laid end to end along the dimension named above; an argument that names none is the same for every part. Nothing has to cross between parts.
Inputs may be any that keep to these rules, and one draw needn't show every extreme that they name: `routes`: each row names two different experts; of the 64 tokens of one index of attn (aligned blocks of rows) at most 48 name any one expert, a bound that some block reaches of them. `lengths`: they sum to 256, and the longest has exactly 128 tokens.
All inputs are finite; a program needn't handle non-finite values.
Results may differ from the reference program's by a relative error of at most 0.008.
Values may be sent and summed in bfloat16 or wider, within the bound.
A program may use at most 192 MiB of HBM per device.

```python
import math
import jax
import jax.numpy as jnp
import numpy as np
from jax import lax

D = 6144
QH = 48
KVH = 8
HD = 128
FF = 8192
SEQS = 4
TOK_DEV = 64
EXPERTS = 4
TOKENS = 256
CAP = 48
N_ATTN = 4


def draw_queries(key, part):
    key = jax.random.fold_in(key, 21)
    result = jnp.clip(jax.random.normal(key, (TOKENS, QH * HD), jnp.float32), -5.0, 5.0)
    return result.astype(jnp.bfloat16)


def draw_keys(key, part):
    key = jax.random.fold_in(key, 22)
    result = jnp.clip(jax.random.normal(key, (TOKENS, KVH * HD), jnp.float32), -5.0, 5.0)
    return result.astype(jnp.bfloat16)


def place_ends(entries, own_key, smallest, largest):
    index_at = [jax.random.randint(jax.random.fold_in(own_key, axis), (), 0, length) for axis, length in enumerate(entries.shape)]
    longest = entries.shape.index(max(entries.shape))
    neighbour = index_at[:longest] + [(index_at[longest] + 1) % entries.shape[longest]] + index_at[longest + 1:]
    return entries.at[tuple(index_at)].set(smallest).at[tuple(neighbour)].set(largest)


def block_scale(rng, dims, pieces, low, top_value):
    gain, own = 1.0, jax.random.fold_in(rng, 6)
    for axis_at, blocks in pieces:
        draws = jnp.exp(jax.random.uniform(jax.random.fold_in(own, axis_at), (blocks,), jnp.float32, low / len(pieces), top_value / len(pieces)))
        gain = gain * jnp.repeat(draws, dims[axis_at] // blocks).reshape([-1 if axis == axis_at else 1 for axis in range(len(dims))])
    return gain


def split_up(number_of, total, most, slope):
    loads = [(1 << 20) // math.isqrt(grade ** slope) + 1 for grade in range(2, number_of + 1)]
    spare, counts = total - most - (number_of - 1), [1] * (number_of - 1)
    while spare > 0:
        candidates = [i for i in range(number_of - 1) if counts[i] < most]
        mass, left = sum([loads[i] for i in candidates]), spare
        for i in candidates:
            extra = min(most - counts[i], max(1, left * loads[i] // mass), spare)
            counts[i] = counts[i] + extra
            spare = spare - extra
    return np.array([most] + counts)


def uneven(rng, number_of, total, limit, lean):
    if number_of == 2:
        one = jax.random.randint(rng, (), max(1, total - limit), min(limit, total - 1) + 1)
        return jnp.stack([one, total - one])
    tallies = jnp.asarray(split_up(number_of, total, limit, lean), jnp.int32)
    couples = (number_of - 1) // 2
    giver, sink = tallies[1:1 + 2 * couples:2], tallies[2:2 + 2 * couples:2]
    margin = jnp.minimum(giver - 1, limit - sink)
    passed = jax.random.randint(jax.random.fold_in(rng, 1), (couples,), 0, 1 << 20) % (margin + 1)
    tallies = tallies.at[1:1 + 2 * couples:2].set(giver - passed).at[2:2 + 2 * couples:2].set(sink + passed)
    return tallies[jax.random.permutation(jax.random.fold_in(rng, 2), number_of)]


def assign_block(rng, own, number, rows, count, top, reach, skew):
    sequence = jax.random.permutation(rng, count)
    heavy_load, common = portions_of(count, rows * top, reach, skew, True), portions_of(count, rows * top, reach, skew, False)
    places = jnp.arange(count)

    def named(sizes, rotation):
        used = int((sizes > 0).sum())
        fixed = max(1, used // 4)
        moved = fixed + (places - fixed + rotation * (used - fixed)) % max(1, count - fixed)
        return jnp.zeros((count,), jnp.int32).at[sequence[jnp.where(places < fixed, places, moved)]].set(jnp.asarray(sizes, jnp.int32))

    sizes = jnp.where(number % 4 == 0, named(heavy_load, number // 4), named(common, number - number // 4 - 1))
    mixed = jax.random.permutation(jax.random.fold_in(own, 3), count)
    source_of, taker = mixed[0:count // 2 * 2:2], mixed[1:count // 2 * 2:2]
    room = jnp.minimum(sizes[source_of] - 1, reach - sizes[taker]) // 2
    room = jnp.where((source_of == sequence[0]) | (taker == sequence[0]) | (sizes[taker] == 0), 0, jnp.maximum(room, 0))
    moved = jax.random.randint(jax.random.fold_in(own, 4), (count // 2,), 0, 1 << 20) % (room + 1)
    sizes = sizes.at[source_of].add(-moved).at[taker].add(moved)
    items = jnp.searchsorted(jnp.cumsum(sizes), jnp.arange(rows * top), side="right").astype(jnp.int32)
    table = items.reshape(top, rows).T
    table = table[jax.random.permutation(jax.random.fold_in(own, 1), rows)]
    rotation = jax.random.randint(jax.random.fold_in(own, 2), (rows, 1), 0, top)
    return jnp.take_along_axis(table, (jnp.arange(top)[None, :] + rotation) % top, axis=1)


def portions_of(number_of, total, limit, slope, full):
    weights = [(1 << 20) // math.isqrt(rank ** slope) + 1 for rank in range(1, number_of + 1)]
    largest = limit if full else min(limit, max(-(-total // number_of), total * weights[0] // sum(weights)))
    least = 1 if total - largest >= number_of - 1 else 0
    counts, surplus = [largest] + [least] * (number_of - 1), total - largest - least * (number_of - 1)
    while surplus > 0:
        free = [i for i in range(1, number_of) if counts[i] < largest] or [i for i in range(1, number_of) if counts[i] < limit]
        mass, budget = sum([weights[i] for i in free]), surplus
        for i in free:
            addition = min(limit - counts[i], max(1, budget * weights[i] // mass), surplus)
            counts[i] = counts[i] + addition
            surplus = surplus - addition
    return np.array(counts)


def bell_draw(own_key, shape, deviation, reach, cuts=(), kind=jnp.bfloat16):
    drawn = deviation * jax.random.normal(own_key, shape, jnp.float32)
    if cuts:
        drawn = drawn * block_scale(own_key, shape, cuts, -0.22, 0.18)
    return jnp.clip(drawn, -reach, reach).astype(kind)


def setup_inputs(seed: int = 0, part: int = 0) -> dict:
    splits = jax.random.split(jax.random.key(seed), 12)
    own_keys = jax.random.split(jax.random.fold_in(splits[11], part), 12)
    hidden_in = bell_draw(own_keys[0], (TOKENS, D), 1.0, 6.0, ((0, 4),))
    queries = draw_queries(jax.random.fold_in(jax.random.fold_in(splits[11], part), 71), part)
    keys = draw_keys(jax.random.fold_in(jax.random.fold_in(splits[11], part), 71), part)
    values = bell_draw(own_keys[3], (TOKENS, KVH * HD), 1.0, 6.0, ((0, 4), (1, 4)))
    norm_gain = jnp.clip(1.0 + 0.18 * jax.random.normal(splits[4], (D,), jnp.float32), 0.099609375, 1.8984375).astype(jnp.bfloat16)
    routes_keys = jax.random.split(jax.random.fold_in(own_keys[5], 1), TOKENS // TOK_DEV)
    routes_turns = jax.random.permutation(jax.random.fold_in(own_keys[5], 3), TOKENS // TOK_DEV)
    routes = jax.vmap(lambda own, number: assign_block(jax.random.fold_in(own_keys[5], 2), own, number, TOK_DEV, EXPERTS, 2, CAP, 2))(routes_keys, routes_turns).reshape((TOKENS, 2))
    gate_codes = place_ends(jax.random.randint(own_keys[6], (TOKENS, 2), 1, 256), jax.random.fold_in(own_keys[6], 1), 1, 255).astype(jnp.int32)
    lengths = uneven(own_keys[7], SEQS, TOKENS, TOKENS // 2, 2).astype(jnp.int32)
    w_gate = bell_draw(splits[8], (EXPERTS, D, FF), D ** -0.5, 0.078125, ((0, 4), (2, 4)))
    w_up = bell_draw(splits[9], (EXPERTS, D, FF), D ** -0.5, 0.078125, ((0, 4), (2, 4)))
    w_down = bell_draw(splits[10], (EXPERTS, FF, D), FF ** -0.5, 0.0625, ((0, 4), (1, 4)))
    return {"hidden_in": hidden_in, "queries": queries, "keys": keys, "values": values, "norm_gain": norm_gain, "routes": routes, "gate_codes": gate_codes, "lengths": lengths, "w_gate": w_gate, "w_up": w_up, "w_down": w_down}


NEG_FILL = -1e+30

def doc_index(position, lengths):
    bounds = jnp.cumsum(lengths)
    return lax.optimization_barrier(jnp.sum((position[:, None] >= bounds[None, :]).astype(jnp.int32), axis=1))

def head_block(query_block, key_block, value_block, allowed):
    scores = jnp.einsum('qgd,kd->gqk', query_block, key_block) * (1.0 / math.sqrt(HD))
    scores = jnp.where(allowed[None], scores, NEG_FILL)
    row_top = lax.optimization_barrier(jnp.max(scores, axis=2, keepdims=True))
    weights = jnp.where(allowed[None], jnp.exp(scores - row_top), jnp.float32(0.0))
    totals = lax.optimization_barrier(jnp.sum(weights, axis=2))
    rounded = lax.optimization_barrier(weights.astype(jnp.bfloat16)).astype(jnp.float32)
    numerator = jnp.einsum('gqk,kd->qgd', rounded, value_block)
    return numerator / jnp.transpose(totals)[:, :, None]

def expert_output(normed, chosen, gate_w, up_w, down_w):
    slots = N_ATTN * CAP
    order = jnp.argsort(jnp.where(chosen, 0, 1).astype(jnp.int32), stable=True)[:slots]
    kept = chosen[order].astype(jnp.float32)
    rows = normed[order]
    gate = jnp.dot(rows, gate_w, preferred_element_type=jnp.float32)
    up_val = jnp.dot(rows, up_w, preferred_element_type=jnp.float32)
    active = (jax.nn.silu(gate) * up_val).astype(jnp.bfloat16)
    block = FF // N_ATTN

    def add_block(index, accum):
        begin = (index * block).astype(jnp.int32)
        part_act = lax.dynamic_slice_in_dim(active, begin, block, 1)
        part_w = lax.dynamic_slice_in_dim(down_w, begin, block, 0)
        partial_value = jnp.dot(part_act, part_w, preferred_element_type=jnp.float32).astype(jnp.bfloat16)
        return accum + lax.optimization_barrier(partial_value).astype(jnp.float32)
    accum = lax.fori_loop(0, N_ATTN, add_block, jnp.zeros((slots, D), jnp.float32))
    return (order, accum * kept[:, None])

def reference(hidden_in, queries, keys, values, norm_gain, routes, gate_codes, lengths, w_gate, w_up, w_down):
    position = jnp.arange(TOKENS, dtype=jnp.int32)
    doc_of = doc_index(position, lengths)
    allowed = (doc_of[:, None] == doc_of[None, :]) & (position[None, :] <= position[:, None])
    per_group = QH // KVH
    query_heads = jnp.transpose(queries.astype(jnp.float32).reshape(TOKENS, KVH, per_group, HD), (1, 0, 2, 3))
    key_heads = jnp.transpose(keys.astype(jnp.float32).reshape(TOKENS, KVH, HD), (1, 0, 2))
    value_heads = jnp.transpose(values.astype(jnp.float32).reshape(TOKENS, KVH, HD), (1, 0, 2))
    outputs = lax.map(lambda parts: head_block(parts[0], parts[1], parts[2], allowed), (query_heads, key_heads, value_heads))
    attended = jnp.transpose(outputs, (1, 0, 2, 3)).reshape(TOKENS, QH * HD).astype(jnp.bfloat16)
    residual = hidden_in.astype(jnp.float32) + lax.optimization_barrier(attended).astype(jnp.float32)
    scale_row = lax.rsqrt(lax.optimization_barrier(jnp.mean(residual * residual, axis=1, keepdims=True)) + 1e-05)
    normed = (residual * scale_row * norm_gain.astype(jnp.float32)[None, :]).astype(jnp.bfloat16)
    codes = gate_codes.astype(jnp.float32)
    gate_share = codes / lax.optimization_barrier(jnp.sum(codes, axis=1, keepdims=True))
    moe = jnp.zeros((TOKENS, D), jnp.float32)
    for expert_id in range(EXPERTS):
        route_hits = routes == expert_id
        chosen = jnp.any(route_hits, axis=1)
        route_weight = lax.optimization_barrier(jnp.sum(jnp.where(route_hits, gate_share, jnp.float32(0.0)), axis=1))
        order, expert_rows = expert_output(normed, chosen, w_gate[expert_id], w_up[expert_id], w_down[expert_id])
        moe = moe.at[order].add(expert_rows * route_weight[order][:, None])
    return (residual + moe).astype(jnp.bfloat16)
```

```python
import functools
import math

import jax
import jax.numpy as jnp
from jax import lax
from jax.experimental import pallas as pl
from jax.experimental.pallas import tpu as pltpu
from jax.sharding import PartitionSpec as P

QH = 48
KVH = 8
HD = 128


NEG_FILL = -1e30


def local(
    hidden_in, queries, keys, values, norm_gain, routes, gate_codes, lengths, w_gate, w_up, w_down
):
    tok_rows = queries.shape[0]
    per_group = QH // KVH
    kv_local = keys.shape[1] // HD
    whole_keys, whole_values = (
        lax.all_gather(keys, "attn", axis=0, tiled=True),
        lax.all_gather(values, "attn", axis=0, tiled=True),
    )
    all_rows_count = whole_keys.shape[0]
    first_row = lax.axis_index("attn") * tok_rows
    query_pos = first_row + jnp.arange(tok_rows, dtype=jnp.int32)
    key_pos = jnp.arange(all_rows_count, dtype=jnp.int32)
    bounds = jnp.cumsum(lengths)
    query_doc = jnp.sum((query_pos[:, None] >= bounds[None, :]).astype(jnp.int32), axis=1)
    key_doc = jnp.sum((key_pos[:, None] >= bounds[None, :]).astype(jnp.int32), axis=1)
    allowed = (query_doc[:, None] == key_doc[None, :]) & (key_pos[None, :] <= query_pos[:, None])
    query_heads = queries.reshape(tok_rows, kv_local, per_group, HD)
    key_heads = whole_keys.reshape(all_rows_count, kv_local, HD)
    value_heads = whole_values.reshape(all_rows_count, kv_local, HD)
    scores = jnp.einsum(
        "qhgd,khd->hgqk", query_heads, key_heads, preferred_element_type=jnp.float32
    ) * (1.0 / math.sqrt(HD))
    scores = jnp.where(allowed[None, None], scores, NEG_FILL)
    row_top = jnp.max(scores, axis=3, keepdims=True)
    weights = jnp.where(allowed[None, None], jnp.exp(scores - row_top), jnp.float32(0.0))
    totals = jnp.sum(weights, axis=3)
    numerator = jnp.einsum(
        "hgqk,khd->qhgd",
        weights.astype(jnp.bfloat16),
        value_heads,
        preferred_element_type=jnp.float32,
    )
    attended = (numerator / jnp.transpose(totals, (2, 0, 1))[:, :, :, None]).astype(jnp.bfloat16)
    attended = attended.reshape(tok_rows, kv_local * per_group * HD)
    full_heads = lax.all_gather(attended, "expert", axis=1, tiled=True)
    residual = hidden_in.astype(jnp.float32) + full_heads.astype(jnp.float32)
    scale_row = lax.rsqrt(jnp.mean(residual * residual, axis=1, keepdims=True) + 1e-05)
    normed = (residual * scale_row * norm_gain.astype(jnp.float32)[None, :]).astype(jnp.bfloat16)
    codes = gate_codes.astype(jnp.float32)
    gate_share = codes / jnp.sum(codes, axis=1, keepdims=True)
    expert_base = lax.axis_index("expert") * w_gate.shape[0]
    route_hits = routes == expert_base + 0
    chosen = jnp.any(route_hits, axis=1)
    route_weight = jnp.sum(jnp.where(route_hits, gate_share, jnp.float32(0.0)), axis=1)
    gate_w = w_gate[0]
    up_w = w_up[0]
    down_w = w_down[0]
    masked = jnp.where(chosen[:, None], normed, jnp.zeros_like(normed))
    block_rows = lax.all_gather(masked, "attn", axis=0, tiled=True)
    gate = jnp.dot(block_rows, gate_w, preferred_element_type=jnp.float32)
    up_val = jnp.dot(block_rows, up_w, preferred_element_type=jnp.float32)
    activated = (jax.nn.silu(gate) * up_val).astype(jnp.bfloat16)
    routed = lax.psum_scatter(
        jnp.dot(activated, down_w, preferred_element_type=jnp.float32).astype(jnp.bfloat16),
        "attn",
        scatter_dimension=0,
        tiled=True,
    ).astype(jnp.float32)
    combined = route_weight[:, None] * routed
    col_width = combined.shape[1] // lax.axis_size("expert")
    col_start = lax.axis_index("expert") * col_width
    full_sum = lax.psum(combined.astype(jnp.bfloat16), "expert").astype(jnp.float32)
    own_share = lax.dynamic_slice_in_dim(full_sum, col_start, col_width, 1)
    own_resid = lax.dynamic_slice_in_dim(residual, col_start, col_width, 1)
    return (own_resid + own_share).astype(jnp.bfloat16)


MESH = pl.DeviceIdType.MESH
SLOTS = 14
CW = 256


def remote(src, dst, send, recv, dev):
    return pltpu.make_async_remote_copy(
        src_ref=src, dst_ref=dst, send_sem=send, recv_sem=recv, device_id=dev, device_id_type=MESH
    )


def fused_kernel(
    nz, q_ref, k_ref, v_ref, gain_ref, routes_ref, codes_ref, len_ref, hid_hbm, wg_hbm, wu_hbm, wd_hbm,
    out_ref,
    wbuf, kall, vall, hid, res, gall, meta, ssq, act, part, rcore, rx, rz,
    wsem, hsem, kv_s, kv_r, q_s, q_r, m_s, m_r, gz_s, gz_r, gx_s, gx_r, gc_s, gc_r,
    pc_s, pc_r, px_s, px_r, pz_s, pz_r,
):
    y = lax.axis_index("groups")
    z = lax.axis_index("attn")
    e = lax.axis_index("expert")
    xx, cc = e // 2, e % 2
    tok, width = q_ref.shape
    rows = nz * tok
    ffl = act.shape[1]
    n_pair = ffl // CW
    n_chunks = 3 * n_pair
    per_slice = n_pair // 4
    three = wbuf.shape[1] // ffl
    ex, ec, ed = (1 - xx) * 2 + cc, xx * 2 + 1 - cc, (1 - xx) * 2 + 1 - cc
    to_x, to_c = (y, z, ex), (y, z, ec)
    order = [ed, ec, ex, e]

    def rowsof(zi):
        return pl.ds(pl.multiple_of(zi * tok, tok), tok)

    def up_to(d):
        return lax.rem(z + d, nz)

    def down_to(d):
        return lax.rem(z + nz - d, nz)

    def gate_copy(j, slot):
        return pltpu.make_async_copy(
            wg_hbm.at[0, :, pl.ds(pl.multiple_of(j * CW, CW), CW)], wbuf.at[slot], wsem.at[slot, 0]
        )

    def up_copy(j, slot):
        return pltpu.make_async_copy(
            wu_hbm.at[0, :, pl.ds(pl.multiple_of(j * CW, CW), CW)], wbuf.at[slot], wsem.at[slot, 0]
        )

    def down_copies(k, slot):
        pos = k // per_slice
        ep = jnp.where(pos == 0, ed, jnp.where(pos == 1, ec, jnp.where(pos == 2, ex, e)))
        base = ep * width + (k % per_slice) * (three * CW)
        return [
            pltpu.make_async_copy(
                wd_hbm.at[0, :, pl.ds(pl.multiple_of(base + t * CW, CW), CW)],
                wbuf.at[slot, pl.ds(t * ffl, ffl)],
                wsem.at[slot, t],
            )
            for t in range(three)
        ]

    hcopy = pltpu.make_async_copy(
        hid_hbm.at[:, pl.ds(pl.multiple_of(e * width, width), width)], hid, hsem
    )
    hcopy.start()

    @pl.loop(0, SLOTS // 2)
    def _(j):
        gate_copy(j, 2 * j).start()
        up_copy(j, 2 * j + 1).start()

    barrier = pltpu.get_barrier_semaphore()
    peers = [(y, up_to(d), e) for d in range(1, nz)] + [(y, z, ex), (y, z, ec), (y, z, ed)]
    for dev in peers:
        pl.semaphore_signal(barrier, inc=1, device_id=dev, device_id_type=MESH)
    pl.semaphore_wait(barrier, len(peers))

    kv = []
    for d in range(1, nz):
        dev = (y, up_to(d), e)
        for i, (a, b) in enumerate(((k_ref, kall), (v_ref, vall))):
            cp = remote(a, b.at[rowsof(z)], kv_s.at[i, d], kv_r.at[i, d], dev)
            cp.start()
            kv.append(cp)
    kall[rowsof(z), :] = k_ref[...]
    vall[rowsof(z), :] = v_ref[...]

    lane = lax.broadcasted_iota(jnp.int32, (tok, 128), 1)
    codes = codes_ref[...].astype(jnp.float32)
    share = codes / (codes[:, 0:1] + codes[:, 1:2])
    routes = routes_ref[...]
    wts = jnp.where(routes[:, 0:1] == lane, share[:, 0:1], 0.0) + jnp.where(
        routes[:, 1:2] == lane, share[:, 1:2], 0.0
    )

    qpos = z * tok + lax.broadcasted_iota(jnp.int32, (tok, rows), 0)
    kpos = lax.broadcasted_iota(jnp.int32, (tok, rows), 1)
    qdoc = jnp.zeros((tok, rows), jnp.int32)
    kdoc = jnp.zeros((tok, rows), jnp.int32)
    bound = jnp.int32(0)
    for s in range(len_ref.shape[0]):
        bound = bound + len_ref[s]
        qdoc = qdoc + (qpos >= bound).astype(jnp.int32)
        kdoc = kdoc + (kpos >= bound).astype(jnp.int32)
    allowed = (qdoc == kdoc) & (kpos <= qpos)

    for cp in kv:
        cp.wait_recv()
    hcopy.wait()

    per_group = QH // KVH
    total = jnp.zeros((tok, 1), jnp.float32)
    for h in range(width // HD):
        g = h // per_group
        cols = slice(h * HD, (h + 1) * HD)
        gcols = slice(g * HD, (g + 1) * HD)
        sc = lax.dot_general(
            q_ref[:, cols], kall[:, gcols], (((1,), (1,)), ((), ())),
            preferred_element_type=jnp.float32,
        ) * (1.0 / math.sqrt(HD))
        sc = jnp.where(allowed, sc, NEG_FILL)
        top = jnp.max(sc, axis=1, keepdims=True)
        w = jnp.where(allowed, jnp.exp(sc - top), 0.0)
        tot = jnp.sum(w, axis=1, keepdims=True)
        num = jnp.dot(w.astype(jnp.bfloat16), vall[:, gcols], preferred_element_type=jnp.float32)
        att = (num / tot).astype(jnp.bfloat16)
        r = hid[:, cols].astype(jnp.float32) + att.astype(jnp.float32)
        res[:, cols] = r
        total = total + jnp.sum(r * r, axis=1, keepdims=True)
        gn = gain_ref[:, pl.ds(pl.multiple_of(e * width + h * HD, HD), HD)].astype(jnp.float32)
        gall[e, rowsof(z), cols] = (r * gn).astype(jnp.bfloat16)

    own = gall.at[e, rowsof(z)]
    sends = []
    gz = []
    ssq[0] = jnp.broadcast_to(total, (tok, 128))
    qc = []
    for i, pe in enumerate((ex, ec, ed)):
        cp = remote(ssq.at[0], ssq.at[i + 1], q_s.at[i], q_r.at[i], (y, z, pe))
        cp.start()
        qc.append(cp)
    for d in range(1, nz):
        cp = remote(own, own, gz_s.at[d], gz_r.at[d], (y, up_to(d), e))
        cp.start()
        gz.append(cp)

    def forward(zi, d):
        blk = gall.at[e, rowsof(zi)]
        a = remote(blk, blk, gx_s.at[d], gx_r.at[d], to_x)
        a.start()
        b = remote(blk, blk, gc_s.at[0, d], gc_r.at[0, d], to_c)
        b.start()
        sends.extend([a, b])

    forward(z, 0)
    for cp in qc:
        cp.wait_recv()
    ms = ssq[0] + ssq[1] + ssq[2] + ssq[3]
    scale = lax.rsqrt(ms * (1.0 / (4 * width)) + 1e-05)
    meta[rowsof(z), :] = jnp.where(lane == 4, scale, wts)
    mc = []
    for d in range(1, nz):
        blk = meta.at[rowsof(z)]
        cp = remote(blk, blk, m_s.at[d], m_r.at[d], (y, up_to(d), e))
        cp.start()
        mc.append(cp)
    for d in range(1, nz):
        gz[d - 1].wait_recv()
        forward(down_to(d), d)
    for d in range(nz):
        zi = down_to(d)
        blk = gall.at[ex, rowsof(zi)]
        remote(blk, blk, gx_s.at[d], gx_r.at[d], to_x).wait_recv()
        b = remote(blk, blk, gc_s.at[1, d], gc_r.at[1, d], to_c)
        b.start()
        sends.append(b)
    for cp in mc:
        cp.wait_recv()
    for d in range(nz):
        zi = down_to(d)
        for i, pe in enumerate((ec, ed)):
            blk = gall.at[pe, rowsof(zi)]
            remote(blk, blk, gc_s.at[i, d], gc_r.at[i, d], to_c).wait_recv()

    scol = meta[:, 4:5]
    mlane = lax.broadcasted_iota(jnp.int32, (rows, 128), 1)
    wcol = jnp.sum(jnp.where(mlane == e, meta[...], 0.0), axis=1, keepdims=True)

    def big(slot):
        acc = jnp.zeros((rows, CW), jnp.float32)
        for i in range(4):
            acc = acc + jnp.dot(
                gall[i], wbuf[slot, i * width : (i + 1) * width, :],
                preferred_element_type=jnp.float32,
            )
        return acc

    @pl.loop(0, n_pair)
    def _(j):
        sg = lax.rem(2 * j, SLOTS)
        su = lax.rem(2 * j + 1, SLOTS)
        gate_copy(j, sg).wait()
        gate = big(sg) * scol
        up_copy(j, su).wait()
        upv = big(su) * scol
        hv = (gate / (1.0 + jnp.exp(-gate))) * upv
        act[:, pl.ds(pl.multiple_of(j * CW, CW), CW)] = hv.astype(jnp.bfloat16)
        nxt = 2 * j + SLOTS

        @pl.when(nxt < 2 * n_pair)
        def _():
            gate_copy(nxt // 2, sg).start()
            up_copy(nxt // 2, su).start()

        @pl.when((nxt >= 2 * n_pair) & (nxt < n_chunks))
        def _():
            for cp in down_copies(nxt - 2 * n_pair, sg) + down_copies(nxt + 1 - 2 * n_pair, su):
                cp.start()

    def down_slice(pos):
        @pl.loop(0, per_slice)
        def _(i):
            k = pos * per_slice + i
            slot = lax.rem(2 * n_pair + k, SLOTS)
            for t, cp in enumerate(down_copies(k, slot)):
                cp.wait()
                o = jnp.dot(
                    act[...], wbuf[slot, t * ffl : (t + 1) * ffl, :],
                    preferred_element_type=jnp.float32,
                )
                col = pl.ds(pl.multiple_of((i * three + t) * CW, CW), CW)
                part[pos, :, col] = (o * wcol).astype(jnp.bfloat16)

    pc = []
    for pos in range(2):
        down_slice(pos)
        cp = remote(part.at[pos], rcore.at[pos], pc_s.at[pos], pc_r.at[pos], to_c)
        cp.start()
        pc.append(cp)
    down_slice(2)
    pc[0].wait_recv()
    steps = [2, 1, 3, 0] if nz == 4 else list(range(1, nz)) + [0]
    px = []
    for n, d in enumerate(steps):
        rr = rowsof(up_to(d))
        part[2, rr, :] = (
            part[2, rr, :].astype(jnp.float32) + rcore[0, rr, :].astype(jnp.float32)
        ).astype(jnp.bfloat16)
        cp = remote(part.at[2, rr], rx.at[rr], px_s.at[n], px_r.at[n], to_x)
        cp.start()
        px.append(cp)
    down_slice(3)
    pc[1].wait_recv()
    pz = []
    for n, d in enumerate(steps):
        rr = rowsof(up_to(d))
        px[n].wait_recv()
        sm = (
            part[3, rr, :].astype(jnp.float32)
            + rcore[1, rr, :].astype(jnp.float32)
            + rx[rr, :].astype(jnp.float32)
        )
        if d:
            part[3, rr, :] = sm.astype(jnp.bfloat16)
            cp = remote(part.at[3, rr], rz.at[d - 1], pz_s.at[d], pz_r.at[d], (y, up_to(d), e))
            cp.start()
            pz.append(cp)
        else:
            res[...] = res[...] + sm
    for cp in pz:
        cp.wait_recv()
    fin = res[...]
    for d in range(1, nz):
        fin = fin + rz[d - 1].astype(jnp.float32)
    out_ref[...] = fin.astype(jnp.bfloat16)
    for cp in kv + qc + mc + gz + sends + pc + px + pz:
        cp.wait_send()


def fused(
    hidden_in, queries, keys, values, norm_gain, routes, gate_codes, lengths, w_gate, w_up, w_down
):
    nz = lax.axis_size("attn")
    tok, width = queries.shape
    rows, full, ffl = nz * tok, hidden_in.shape[1], w_gate.shape[2]
    bf, f32, dma = jnp.bfloat16, jnp.float32, pltpu.SemaphoreType.DMA
    vm = pl.BlockSpec(memory_space=pltpu.VMEM)
    hbm = pl.BlockSpec(memory_space=pl.ANY)
    return pl.pallas_call(
        functools.partial(fused_kernel, nz),
        out_shape=jax.ShapeDtypeStruct((tok, width), bf),
        in_specs=[vm] * 6 + [pl.BlockSpec(memory_space=pltpu.SMEM)] + [hbm] * 4,
        out_specs=vm,
        scratch_shapes=[
            pltpu.VMEM((SLOTS, full, CW), bf),
            pltpu.VMEM((rows, keys.shape[1]), bf),
            pltpu.VMEM((rows, keys.shape[1]), bf),
            pltpu.VMEM((tok, width), bf),
            pltpu.VMEM((tok, width), f32),
            pltpu.VMEM((4, rows, width), bf),
            pltpu.VMEM((rows, 128), f32),
            pltpu.VMEM((4, tok, 128), f32),
            pltpu.VMEM((rows, ffl), bf),
            pltpu.VMEM((4, rows, width), bf),
            pltpu.VMEM((2, rows, width), bf),
            pltpu.VMEM((rows, width), bf),
            pltpu.VMEM((nz - 1, tok, width), bf),
            dma((SLOTS, full // ffl)),
            dma,
            dma((2, nz)), dma((2, nz)),
            dma((3,)), dma((3,)),
            dma((nz,)), dma((nz,)),
            dma((nz,)), dma((nz,)),
            dma((nz,)), dma((nz,)),
            dma((2, nz)), dma((2, nz)),
            dma((2,)), dma((2,)),
            dma((nz,)), dma((nz,)),
            dma((nz,)), dma((nz,)),
        ],
        compiler_params=pltpu.CompilerParams(
            collective_id=0, has_side_effects=True, vmem_limit_bytes=62 * 2**20
        ),
    )(
        queries, keys, values, norm_gain.reshape(1, full), routes, gate_codes, lengths,
        hidden_in, w_gate, w_up, w_down,
    )


def fits(mesh, w_gate):
    nz, ffl = mesh.shape["attn"], w_gate.shape[2] // mesh.shape["attn"]
    return nz == 4 and mesh.shape["expert"] == 4 and 3 * ffl == w_gate.shape[1]


def solution(mesh):
    placed = (
        P(("groups", "attn"), None),
        P(("groups", "attn"), "expert"),
        P(("groups", "attn"), "expert"),
        P(("groups", "attn"), "expert"),
        P(),
        P(("groups", "attn"), None),
        P(("groups", "attn"), None),
        P("groups"),
        P("expert", None, "attn"),
        P("expert", None, "attn"),
        P("expert", "attn", None),
    )

    def run(*args):
        return jax.shard_map(
            fused if fits(mesh, args[8]) else local,
            mesh=mesh,
            in_specs=placed,
            out_specs=P(("groups", "attn"), "expert"),
            check_vma=False,
        )(*args)

    return run
```

```python
import functools
import math

import jax
import jax.numpy as jnp
from jax import lax
from jax.experimental import pallas as pl
from jax.experimental.pallas import tpu as pltpu
from jax.sharding import PartitionSpec as P

QH = 48
KVH = 8
HD = 128


NEG_FILL = -1e30


def local(
    hidden_in, queries, keys, values, norm_gain, routes, gate_codes, lengths, w_gate, w_up, w_down
):
    tok_rows = queries.shape[0]
    per_group = QH // KVH
    kv_local = keys.shape[1] // HD
    whole_keys, whole_values = (
        lax.all_gather(keys, "attn", axis=0, tiled=True),
        lax.all_gather(values, "attn", axis=0, tiled=True),
    )
    all_rows_count = whole_keys.shape[0]
    first_row = lax.axis_index("attn") * tok_rows
    query_pos = first_row + jnp.arange(tok_rows, dtype=jnp.int32)
    key_pos = jnp.arange(all_rows_count, dtype=jnp.int32)
    bounds = jnp.cumsum(lengths)
    query_doc = jnp.sum((query_pos[:, None] >= bounds[None, :]).astype(jnp.int32), axis=1)
    key_doc = jnp.sum((key_pos[:, None] >= bounds[None, :]).astype(jnp.int32), axis=1)
    allowed = (query_doc[:, None] == key_doc[None, :]) & (key_pos[None, :] <= query_pos[:, None])
    query_heads = queries.reshape(tok_rows, kv_local, per_group, HD)
    key_heads = whole_keys.reshape(all_rows_count, kv_local, HD)
    value_heads = whole_values.reshape(all_rows_count, kv_local, HD)
    scores = jnp.einsum(
        "qhgd,khd->hgqk", query_heads, key_heads, preferred_element_type=jnp.float32
    ) * (1.0 / math.sqrt(HD))
    scores = jnp.where(allowed[None, None], scores, NEG_FILL)
    row_top = jnp.max(scores, axis=3, keepdims=True)
    weights = jnp.where(allowed[None, None], jnp.exp(scores - row_top), jnp.float32(0.0))
    totals = jnp.sum(weights, axis=3)
    numerator = jnp.einsum(
        "hgqk,khd->qhgd",
        weights.astype(jnp.bfloat16),
        value_heads,
        preferred_element_type=jnp.float32,
    )
    attended = (numerator / jnp.transpose(totals, (2, 0, 1))[:, :, :, None]).astype(jnp.bfloat16)
    attended = attended.reshape(tok_rows, kv_local * per_group * HD)
    full_heads = lax.all_gather(attended, "expert", axis=1, tiled=True)
    residual = hidden_in.astype(jnp.float32) + full_heads.astype(jnp.float32)
    scale_row = lax.rsqrt(jnp.mean(residual * residual, axis=1, keepdims=True) + 1e-05)
    normed = (residual * scale_row * norm_gain.astype(jnp.float32)[None, :]).astype(jnp.bfloat16)
    codes = gate_codes.astype(jnp.float32)
    gate_share = codes / jnp.sum(codes, axis=1, keepdims=True)
    expert_base = lax.axis_index("expert") * w_gate.shape[0]
    route_hits = routes == expert_base + 0
    chosen = jnp.any(route_hits, axis=1)
    route_weight = jnp.sum(jnp.where(route_hits, gate_share, jnp.float32(0.0)), axis=1)
    gate_w = w_gate[0]
    up_w = w_up[0]
    down_w = w_down[0]
    masked = jnp.where(chosen[:, None], normed, jnp.zeros_like(normed))
    block_rows = lax.all_gather(masked, "attn", axis=0, tiled=True)
    gate = jnp.dot(block_rows, gate_w, preferred_element_type=jnp.float32)
    up_val = jnp.dot(block_rows, up_w, preferred_element_type=jnp.float32)
    activated = (jax.nn.silu(gate) * up_val).astype(jnp.bfloat16)
    routed = lax.psum_scatter(
        jnp.dot(activated, down_w, preferred_element_type=jnp.float32).astype(jnp.bfloat16),
        "attn",
        scatter_dimension=0,
        tiled=True,
    ).astype(jnp.float32)
    combined = route_weight[:, None] * routed
    col_width = combined.shape[1] // lax.axis_size("expert")
    col_start = lax.axis_index("expert") * col_width
    full_sum = lax.psum(combined.astype(jnp.bfloat16), "expert").astype(jnp.float32)
    own_share = lax.dynamic_slice_in_dim(full_sum, col_start, col_width, 1)
    own_resid = lax.dynamic_slice_in_dim(residual, col_start, col_width, 1)
    return (own_resid + own_share).astype(jnp.bfloat16)


MESH = pl.DeviceIdType.MESH
SLOTS = 6
CW = 512


def remote(src, dst, send, recv, dev):
    return pltpu.make_async_remote_copy(
        src_ref=src, dst_ref=dst, send_sem=send, recv_sem=recv, device_id=dev, device_id_type=MESH
    )


def fused_kernel(
    nz, q_ref, k_ref, v_ref, gain_ref, routes_ref, codes_ref, len_ref, hid_hbm, wg_hbm, wu_hbm, wd_hbm,
    out_ref,
    wbuf, kall, vall, hid, res, gall, meta, ssq, act, part, rcore, rx, rz,
    wsem, hsem, kv_s, kv_r, q_s, q_r, m_s, m_r, gz_s, gz_r, gx_s, gx_r, gc_s, gc_r,
    pc_s, pc_r, px_s, px_r, pz_s, pz_r,
):
    y = lax.axis_index("groups")
    z = lax.axis_index("attn")
    e = lax.axis_index("expert")
    xx, cc = e // 2, e % 2
    tok, width = q_ref.shape
    rows = nz * tok
    ffl = act.shape[1]
    n_pair = ffl // CW
    n_chunks = 3 * n_pair
    per_slice = n_pair // 4
    three = wbuf.shape[1] // ffl
    ex, ec, ed = (1 - xx) * 2 + cc, xx * 2 + 1 - cc, (1 - xx) * 2 + 1 - cc
    to_x, to_c = (y, z, ex), (y, z, ec)
    order = [ed, ec, ex, e]

    def rowsof(zi):
        return pl.ds(pl.multiple_of(zi * tok, tok), tok)

    def up_to(d):
        return lax.rem(z + d, nz)

    def down_to(d):
        return lax.rem(z + nz - d, nz)

    def gate_copy(j, slot):
        return pltpu.make_async_copy(
            wg_hbm.at[0, :, pl.ds(pl.multiple_of(j * CW, CW), CW)], wbuf.at[slot], wsem.at[slot, 0]
        )

    def up_copy(j, slot):
        return pltpu.make_async_copy(
            wu_hbm.at[0, :, pl.ds(pl.multiple_of(j * CW, CW), CW)], wbuf.at[slot], wsem.at[slot, 0]
        )

    def down_copies(k, slot):
        pos = k // per_slice
        ep = jnp.where(pos == 0, ed, jnp.where(pos == 1, ec, jnp.where(pos == 2, ex, e)))
        base = ep * width + (k % per_slice) * (three * CW)
        return [
            pltpu.make_async_copy(
                wd_hbm.at[0, :, pl.ds(pl.multiple_of(base + t * CW, CW), CW)],
                wbuf.at[slot, pl.ds(t * ffl, ffl)],
                wsem.at[slot, t],
            )
            for t in range(three)
        ]

    hcopy = pltpu.make_async_copy(
        hid_hbm.at[:, pl.ds(pl.multiple_of(e * width, width), width)], hid, hsem
    )
    hcopy.start()

    @pl.loop(0, SLOTS // 2)
    def _(j):
        gate_copy(j, 2 * j).start()
        up_copy(j, 2 * j + 1).start()

    barrier = pltpu.get_barrier_semaphore()
    peers = [(y, up_to(d), e) for d in range(1, nz)] + [(y, z, ex), (y, z, ec), (y, z, ed)]
    for dev in peers:
        pl.semaphore_signal(barrier, inc=1, device_id=dev, device_id_type=MESH)
    pl.semaphore_wait(barrier, len(peers))

    kv = []
    for d in range(1, nz):
        dev = (y, up_to(d), e)
        for i, (a, b) in enumerate(((k_ref, kall), (v_ref, vall))):
            cp = remote(a, b.at[rowsof(z)], kv_s.at[i, d], kv_r.at[i, d], dev)
            cp.start()
            kv.append(cp)
    kall[rowsof(z), :] = k_ref[...]
    vall[rowsof(z), :] = v_ref[...]

    lane = lax.broadcasted_iota(jnp.int32, (tok, 128), 1)
    codes = codes_ref[...].astype(jnp.float32)
    csum = codes[0:1, :] + codes[1:2, :]
    eye = lax.broadcasted_iota(jnp.int32, (tok, tok), 0) == lax.broadcasted_iota(
        jnp.int32, (tok, tok), 1
    )
    wts = jnp.zeros((tok, 128), jnp.float32)
    for x in range(4):
        hit = jnp.where(routes_ref[...] == x, codes, 0.0)
        row = (hit[0:1, :] + hit[1:2, :]) / csum
        col = jnp.sum(jnp.where(eye, row, 0.0), axis=1, keepdims=True)
        wts = wts + jnp.where(lane == x, col, 0.0)

    qpos = z * tok + lax.broadcasted_iota(jnp.int32, (tok, rows), 0)
    kpos = lax.broadcasted_iota(jnp.int32, (tok, rows), 1)
    qdoc = jnp.zeros((tok, rows), jnp.int32)
    kdoc = jnp.zeros((tok, rows), jnp.int32)
    bound = jnp.int32(0)
    for s in range(len_ref.shape[0]):
        bound = bound + len_ref[s]
        qdoc = qdoc + (qpos >= bound).astype(jnp.int32)
        kdoc = kdoc + (kpos >= bound).astype(jnp.int32)
    allowed = (qdoc == kdoc) & (kpos <= qpos)

    for cp in kv:
        cp.wait_recv()
    hcopy.wait()

    per_group = QH // KVH
    total = jnp.zeros((tok, 1), jnp.float32)
    mask = jnp.concatenate([allowed] * per_group, axis=0)
    for g in range(width // HD // per_group):
        gcols = slice(g * HD, (g + 1) * HD)
        heads = [slice(h * HD, (h + 1) * HD) for h in range(g * per_group, (g + 1) * per_group)]
        qs = jnp.concatenate([q_ref[:, c] for c in heads], axis=0)
        sc = lax.dot_general(
            qs, kall[:, gcols], (((1,), (1,)), ((), ())), preferred_element_type=jnp.float32
        ) * (1.0 / math.sqrt(HD))
        sc = jnp.where(mask, sc, NEG_FILL)
        top = jnp.max(sc, axis=1, keepdims=True)
        w = jnp.where(mask, jnp.exp(sc - top), 0.0)
        tot = jnp.sum(w, axis=1, keepdims=True)
        num = jnp.dot(w.astype(jnp.bfloat16), vall[:, gcols], preferred_element_type=jnp.float32)
        att = (num / tot).astype(jnp.bfloat16).astype(jnp.float32)
        for n, cols in enumerate(heads):
            r = hid[:, cols].astype(jnp.float32) + att[n * tok : (n + 1) * tok, :]
            res[:, cols] = r
            total = total + jnp.sum(r * r, axis=1, keepdims=True)
            gn = gain_ref[:, pl.ds(pl.multiple_of(e * width + cols.start, HD), HD)].astype(jnp.float32)
            gall[e, rowsof(z), cols] = (r * gn).astype(jnp.bfloat16)

    own = gall.at[e, rowsof(z)]
    sends = []
    gz = []
    ssq[0] = jnp.broadcast_to(total, (tok, 128))
    qc = []
    for i, pe in enumerate((ex, ec, ed)):
        cp = remote(ssq.at[0], ssq.at[i + 1], q_s.at[i], q_r.at[i], (y, z, pe))
        cp.start()
        qc.append(cp)
    for d in range(1, nz):
        cp = remote(own, own, gz_s.at[d], gz_r.at[d], (y, up_to(d), e))
        cp.start()
        gz.append(cp)

    def forward(zi, d):
        blk = gall.at[e, rowsof(zi)]
        a = remote(blk, blk, gx_s.at[d], gx_r.at[d], to_x)
        a.start()
        b = remote(blk, blk, gc_s.at[0, d], gc_r.at[0, d], to_c)
        b.start()
        sends.extend([a, b])

    forward(z, 0)
    for cp in qc:
        cp.wait_recv()
    ms = ssq[0] + ssq[1] + ssq[2] + ssq[3]
    scale = lax.rsqrt(ms * (1.0 / (4 * width)) + 1e-05)
    meta[rowsof(z), :] = jnp.where(lane == 4, scale, wts)
    mc = []
    for d in range(1, nz):
        blk = meta.at[rowsof(z)]
        cp = remote(blk, blk, m_s.at[d], m_r.at[d], (y, up_to(d), e))
        cp.start()
        mc.append(cp)
    for d in range(1, nz):
        gz[d - 1].wait_recv()
        forward(down_to(d), d)
    for d in range(nz):
        zi = down_to(d)
        blk = gall.at[ex, rowsof(zi)]
        remote(blk, blk, gx_s.at[d], gx_r.at[d], to_x).wait_recv()
        b = remote(blk, blk, gc_s.at[1, d], gc_r.at[1, d], to_c)
        b.start()
        sends.append(b)
    for cp in mc:
        cp.wait_recv()
    for d in range(nz):
        zi = down_to(d)
        for i, pe in enumerate((ec, ed)):
            blk = gall.at[pe, rowsof(zi)]
            remote(blk, blk, gc_s.at[i, d], gc_r.at[i, d], to_c).wait_recv()

    scol = meta[:, 4:5]
    mlane = lax.broadcasted_iota(jnp.int32, (rows, 128), 1)
    wcol = jnp.sum(jnp.where(mlane == e, meta[...], 0.0), axis=1, keepdims=True)

    def big(slot):
        acc = jnp.zeros((rows, CW), jnp.float32)
        for i in range(4):
            acc = acc + jnp.dot(
                gall[i], wbuf[slot, i * width : (i + 1) * width, :],
                preferred_element_type=jnp.float32,
            )
        return acc

    @pl.loop(0, n_pair)
    def _(j):
        sg = lax.rem(2 * j, SLOTS)
        su = lax.rem(2 * j + 1, SLOTS)
        gate_copy(j, sg).wait()
        up_copy(j, su).wait()
        gate = big(sg) * scol
        upv = big(su) * scol
        hv = (gate / (1.0 + jnp.exp(-gate))) * upv
        act[:, pl.ds(pl.multiple_of(j * CW, CW), CW)] = hv.astype(jnp.bfloat16)
        nxt = 2 * j + SLOTS

        @pl.when(nxt < 2 * n_pair)
        def _():
            gate_copy(nxt // 2, sg).start()
            up_copy(nxt // 2, su).start()

        @pl.when((nxt >= 2 * n_pair) & (nxt < n_chunks))
        def _():
            for cp in down_copies(nxt - 2 * n_pair, sg) + down_copies(nxt + 1 - 2 * n_pair, su):
                cp.start()

    def down_slice(pos):
        @pl.loop(0, per_slice)
        def _(i):
            k = pos * per_slice + i
            slot = lax.rem(2 * n_pair + k, SLOTS)
            for t, cp in enumerate(down_copies(k, slot)):
                cp.wait()
                o = jnp.dot(
                    act[...], wbuf[slot, t * ffl : (t + 1) * ffl, :],
                    preferred_element_type=jnp.float32,
                )
                col = pl.ds(pl.multiple_of((i * three + t) * CW, CW), CW)
                part[pos, :, col] = (o * wcol).astype(jnp.bfloat16)

    pc = []
    for pos in range(2):
        down_slice(pos)
        cp = remote(part.at[pos], rcore.at[pos], pc_s.at[pos], pc_r.at[pos], to_c)
        cp.start()
        pc.append(cp)
    down_slice(2)
    pc[0].wait_recv()
    steps = [2, 1, 3, 0] if nz == 4 else list(range(1, nz)) + [0]
    px = []
    for n, d in enumerate(steps):
        rr = rowsof(up_to(d))
        part[2, rr, :] = (
            part[2, rr, :].astype(jnp.float32) + rcore[0, rr, :].astype(jnp.float32)
        ).astype(jnp.bfloat16)
        cp = remote(part.at[2, rr], rx.at[rr], px_s.at[n], px_r.at[n], to_x)
        cp.start()
        px.append(cp)
    down_slice(3)
    pc[1].wait_recv()
    pz = []
    for n, d in enumerate(steps):
        rr = rowsof(up_to(d))
        px[n].wait_recv()
        sm = (
            part[3, rr, :].astype(jnp.float32)
            + rcore[1, rr, :].astype(jnp.float32)
            + rx[rr, :].astype(jnp.float32)
        )
        if d:
            part[3, rr, :] = sm.astype(jnp.bfloat16)
            cp = remote(part.at[3, rr], rz.at[d - 1], pz_s.at[d], pz_r.at[d], (y, up_to(d), e))
            cp.start()
            pz.append(cp)
        else:
            res[...] = res[...] + sm
    for cp in pz:
        cp.wait_recv()
    fin = res[...]
    for d in range(1, nz):
        fin = fin + rz[d - 1].astype(jnp.float32)
    out_ref[...] = fin.astype(jnp.bfloat16)
    for cp in kv + qc + mc + gz + sends + pc + px + pz:
        cp.wait_send()


def fused(
    hidden_in, queries, keys, values, norm_gain, routes, gate_codes, lengths, w_gate, w_up, w_down
):
    nz = lax.axis_size("attn")
    tok, width = queries.shape
    rows, full, ffl = nz * tok, hidden_in.shape[1], w_gate.shape[2]
    bf, f32, dma = jnp.bfloat16, jnp.float32, pltpu.SemaphoreType.DMA
    vm = pl.BlockSpec(memory_space=pltpu.VMEM)
    hbm = pl.BlockSpec(memory_space=pl.ANY)
    return pl.pallas_call(
        functools.partial(fused_kernel, nz),
        out_shape=jax.ShapeDtypeStruct((tok, width), bf),
        in_specs=[vm] * 6 + [pl.BlockSpec(memory_space=pltpu.SMEM)] + [hbm] * 4,
        out_specs=vm,
        scratch_shapes=[
            pltpu.VMEM((SLOTS, full, CW), bf),
            pltpu.VMEM((rows, keys.shape[1]), bf),
            pltpu.VMEM((rows, keys.shape[1]), bf),
            pltpu.VMEM((tok, width), bf),
            pltpu.VMEM((tok, width), f32),
            pltpu.VMEM((4, rows, width), bf),
            pltpu.VMEM((rows, 128), f32),
            pltpu.VMEM((4, tok, 128), f32),
            pltpu.VMEM((rows, ffl), bf),
            pltpu.VMEM((4, rows, width), bf),
            pltpu.VMEM((2, rows, width), bf),
            pltpu.VMEM((rows, width), bf),
            pltpu.VMEM((nz - 1, tok, width), bf),
            dma((SLOTS, full // ffl)),
            dma,
            dma((2, nz)), dma((2, nz)),
            dma((3,)), dma((3,)),
            dma((nz,)), dma((nz,)),
            dma((nz,)), dma((nz,)),
            dma((nz,)), dma((nz,)),
            dma((2, nz)), dma((2, nz)),
            dma((2,)), dma((2,)),
            dma((nz,)), dma((nz,)),
            dma((nz,)), dma((nz,)),
        ],
        compiler_params=pltpu.CompilerParams(
            collective_id=0, has_side_effects=True, vmem_limit_bytes=62 * 2**20
        ),
    )(
        queries, keys, values, norm_gain.reshape(1, full), routes.T, gate_codes.T, lengths,
        hidden_in, w_gate, w_up, w_down,
    )


def fits(mesh, w_gate):
    nz, ffl = mesh.shape["attn"], w_gate.shape[2] // mesh.shape["attn"]
    return nz == 4 and mesh.shape["expert"] == 4 and 3 * ffl == w_gate.shape[1]


def solution(mesh):
    placed = (
        P(("groups", "attn"), None),
        P(("groups", "attn"), "expert"),
        P(("groups", "attn"), "expert"),
        P(("groups", "attn"), "expert"),
        P(),
        P(("groups", "attn"), None),
        P(("groups", "attn"), None),
        P("groups"),
        P("expert", None, "attn"),
        P("expert", None, "attn"),
        P("expert", "attn", None),
    )

    def run(*args):
        return jax.shard_map(
            fused if fits(mesh, args[8]) else local,
            mesh=mesh,
            in_specs=placed,
            out_specs=P(("groups", "attn"), "expert"),
            check_vma=False,
        )(*args)

    return run
```

```python
import functools
import math

import jax
import jax.numpy as jnp
from jax import lax
from jax.experimental import pallas as pl
from jax.experimental.pallas import tpu as pltpu
from jax.sharding import PartitionSpec as P

QH = 48
KVH = 8
HD = 128


NEG_FILL = -1e30


def local(
    hidden_in, queries, keys, values, norm_gain, routes, gate_codes, lengths, w_gate, w_up, w_down
):
    tok_rows = queries.shape[0]
    per_group = QH // KVH
    kv_local = keys.shape[1] // HD
    whole_keys, whole_values = (
        lax.all_gather(keys, "attn", axis=0, tiled=True),
        lax.all_gather(values, "attn", axis=0, tiled=True),
    )
    all_rows_count = whole_keys.shape[0]
    first_row = lax.axis_index("attn") * tok_rows
    query_pos = first_row + jnp.arange(tok_rows, dtype=jnp.int32)
    key_pos = jnp.arange(all_rows_count, dtype=jnp.int32)
    bounds = jnp.cumsum(lengths)
    query_doc = jnp.sum((query_pos[:, None] >= bounds[None, :]).astype(jnp.int32), axis=1)
    key_doc = jnp.sum((key_pos[:, None] >= bounds[None, :]).astype(jnp.int32), axis=1)
    allowed = (query_doc[:, None] == key_doc[None, :]) & (key_pos[None, :] <= query_pos[:, None])
    query_heads = queries.reshape(tok_rows, kv_local, per_group, HD)
    key_heads = whole_keys.reshape(all_rows_count, kv_local, HD)
    value_heads = whole_values.reshape(all_rows_count, kv_local, HD)
    scores = jnp.einsum(
        "qhgd,khd->hgqk", query_heads, key_heads, preferred_element_type=jnp.float32
    ) * (1.0 / math.sqrt(HD))
    scores = jnp.where(allowed[None, None], scores, NEG_FILL)
    row_top = jnp.max(scores, axis=3, keepdims=True)
    weights = jnp.where(allowed[None, None], jnp.exp(scores - row_top), jnp.float32(0.0))
    totals = jnp.sum(weights, axis=3)
    numerator = jnp.einsum(
        "hgqk,khd->qhgd",
        weights.astype(jnp.bfloat16),
        value_heads,
        preferred_element_type=jnp.float32,
    )
    attended = (numerator / jnp.transpose(totals, (2, 0, 1))[:, :, :, None]).astype(jnp.bfloat16)
    attended = attended.reshape(tok_rows, kv_local * per_group * HD)
    full_heads = lax.all_gather(attended, "expert", axis=1, tiled=True)
    residual = hidden_in.astype(jnp.float32) + full_heads.astype(jnp.float32)
    scale_row = lax.rsqrt(jnp.mean(residual * residual, axis=1, keepdims=True) + 1e-05)
    normed = (residual * scale_row * norm_gain.astype(jnp.float32)[None, :]).astype(jnp.bfloat16)
    codes = gate_codes.astype(jnp.float32)
    gate_share = codes / jnp.sum(codes, axis=1, keepdims=True)
    expert_base = lax.axis_index("expert") * w_gate.shape[0]
    route_hits = routes == expert_base + 0
    chosen = jnp.any(route_hits, axis=1)
    route_weight = jnp.sum(jnp.where(route_hits, gate_share, jnp.float32(0.0)), axis=1)
    gate_w = w_gate[0]
    up_w = w_up[0]
    down_w = w_down[0]
    masked = jnp.where(chosen[:, None], normed, jnp.zeros_like(normed))
    block_rows = lax.all_gather(masked, "attn", axis=0, tiled=True)
    gate = jnp.dot(block_rows, gate_w, preferred_element_type=jnp.float32)
    up_val = jnp.dot(block_rows, up_w, preferred_element_type=jnp.float32)
    activated = (jax.nn.silu(gate) * up_val).astype(jnp.bfloat16)
    routed = lax.psum_scatter(
        jnp.dot(activated, down_w, preferred_element_type=jnp.float32).astype(jnp.bfloat16),
        "attn",
        scatter_dimension=0,
        tiled=True,
    ).astype(jnp.float32)
    combined = route_weight[:, None] * routed
    col_width = combined.shape[1] // lax.axis_size("expert")
    col_start = lax.axis_index("expert") * col_width
    full_sum = lax.psum(combined.astype(jnp.bfloat16), "expert").astype(jnp.float32)
    own_share = lax.dynamic_slice_in_dim(full_sum, col_start, col_width, 1)
    own_resid = lax.dynamic_slice_in_dim(residual, col_start, col_width, 1)
    return (own_resid + own_share).astype(jnp.bfloat16)


MESH = pl.DeviceIdType.MESH
SLOTS = 6
CW = 512


def remote(src, dst, send, recv, dev):
    return pltpu.make_async_remote_copy(
        src_ref=src, dst_ref=dst, send_sem=send, recv_sem=recv, device_id=dev, device_id_type=MESH
    )


def fused_kernel(
    nz, q_ref, k_ref, v_ref, gain_ref, routes_ref, codes_ref, len_ref, hid_hbm, wg_hbm, wu_hbm, wd_hbm,
    out_ref,
    wbuf, kall, vall, hid, res, gall, meta, ssq, act, part, rcore, rx, rz, pacc,
    wsem, hsem, kv_s, kv_r, q_s, q_r, m_s, m_r, gz_s, gz_r, gx_s, gx_r, gc_s, gc_r,
    pc_s, pc_r, px_s, px_r, pz_s, pz_r,
):
    y = lax.axis_index("groups")
    z = lax.axis_index("attn")
    e = lax.axis_index("expert")
    xx, cc = e // 2, e % 2
    tok, width = q_ref.shape
    rows = nz * tok
    ffl = act.shape[1]
    n_pair = ffl // CW
    n_chunks = 3 * n_pair
    per_slice = n_pair // 4
    three = wbuf.shape[1] // ffl
    ex, ec, ed = (1 - xx) * 2 + cc, xx * 2 + 1 - cc, (1 - xx) * 2 + 1 - cc
    to_x, to_c = (y, z, ex), (y, z, ec)

    def rowsof(zi):
        return pl.ds(pl.multiple_of(zi * tok, tok), tok)

    def up_to(d):
        return lax.rem(z + d, nz)

    def down_to(d):
        return lax.rem(z + nz - d, nz)

    def gate_copy(j, slot):
        return pltpu.make_async_copy(
            wg_hbm.at[0, :, pl.ds(pl.multiple_of(j * CW, CW), CW)], wbuf.at[slot], wsem.at[slot, 0]
        )

    def up_copy(j, slot):
        return pltpu.make_async_copy(
            wu_hbm.at[0, :, pl.ds(pl.multiple_of(j * CW, CW), CW)], wbuf.at[slot], wsem.at[slot, 0]
        )

    def down_copies(k, slot):
        pos = k // per_slice
        ep = jnp.where(pos == 0, ed, jnp.where(pos == 1, ex, jnp.where(pos == 2, ec, e)))
        base = ep * width + (k % per_slice) * (three * CW)
        return [
            pltpu.make_async_copy(
                wd_hbm.at[0, :, pl.ds(pl.multiple_of(base + t * CW, CW), CW)],
                wbuf.at[slot, pl.ds(t * ffl, ffl)],
                wsem.at[slot, t],
            )
            for t in range(three)
        ]

    hcopy = pltpu.make_async_copy(
        hid_hbm.at[:, pl.ds(pl.multiple_of(e * width, width), width)], hid, hsem
    )
    hcopy.start()

    @pl.loop(0, SLOTS // 2)
    def _(j):
        gate_copy(j, 2 * j).start()
        up_copy(j, 2 * j + 1).start()

    barrier = pltpu.get_barrier_semaphore()
    peers = [(y, up_to(d), e) for d in range(1, nz)] + [(y, z, ex), (y, z, ec), (y, z, ed)]
    for dev in peers:
        pl.semaphore_signal(barrier, inc=1, device_id=dev, device_id_type=MESH)
    pl.semaphore_wait(barrier, len(peers))

    kv = []
    for d in range(1, nz):
        dev = (y, up_to(d), e)
        for i, (a, b) in enumerate(((k_ref, kall), (v_ref, vall))):
            cp = remote(a, b.at[rowsof(z)], kv_s.at[i, d], kv_r.at[i, d], dev)
            cp.start()
            kv.append(cp)
    kall[rowsof(z), :] = k_ref[...]
    vall[rowsof(z), :] = v_ref[...]

    lane = lax.broadcasted_iota(jnp.int32, (tok, 128), 1)
    codes = codes_ref[...].astype(jnp.float32)
    csum = codes[0:1, :] + codes[1:2, :]
    eye = lax.broadcasted_iota(jnp.int32, (tok, tok), 0) == lax.broadcasted_iota(
        jnp.int32, (tok, tok), 1
    )
    wts = jnp.zeros((tok, 128), jnp.float32)
    for x in range(4):
        hit = jnp.where(routes_ref[...] == x, codes, 0.0)
        row = (hit[0:1, :] + hit[1:2, :]) / csum
        col = jnp.sum(jnp.where(eye, row, 0.0), axis=1, keepdims=True)
        wts = wts + jnp.where(lane == x, col, 0.0)

    qpos = z * tok + lax.broadcasted_iota(jnp.int32, (tok, rows), 0)
    kpos = lax.broadcasted_iota(jnp.int32, (tok, rows), 1)
    qdoc = jnp.zeros((tok, rows), jnp.int32)
    kdoc = jnp.zeros((tok, rows), jnp.int32)
    bound = jnp.int32(0)
    for s in range(len_ref.shape[0]):
        bound = bound + len_ref[s]
        qdoc = qdoc + (qpos >= bound).astype(jnp.int32)
        kdoc = kdoc + (kpos >= bound).astype(jnp.int32)
    allowed = (qdoc == kdoc) & (kpos <= qpos)

    for cp in kv:
        cp.wait_recv()
    hcopy.wait()

    per_group = QH // KVH
    total = jnp.zeros((tok, 1), jnp.float32)
    mask = jnp.concatenate([allowed] * per_group, axis=0)
    for g in range(width // HD // per_group):
        gcols = slice(g * HD, (g + 1) * HD)
        heads = [slice(h * HD, (h + 1) * HD) for h in range(g * per_group, (g + 1) * per_group)]
        qs = jnp.concatenate([q_ref[:, c] for c in heads], axis=0)
        sc = lax.dot_general(
            qs, kall[:, gcols], (((1,), (1,)), ((), ())), preferred_element_type=jnp.float32
        ) * (1.0 / math.sqrt(HD))
        sc = jnp.where(mask, sc, NEG_FILL)
        top = jnp.max(sc, axis=1, keepdims=True)
        w = jnp.where(mask, jnp.exp(sc - top), 0.0)
        tot = jnp.sum(w, axis=1, keepdims=True)
        num = jnp.dot(w.astype(jnp.bfloat16), vall[:, gcols], preferred_element_type=jnp.float32)
        att = (num / tot).astype(jnp.bfloat16).astype(jnp.float32)
        for n, cols in enumerate(heads):
            r = hid[:, cols].astype(jnp.float32) + att[n * tok : (n + 1) * tok, :]
            res[:, cols] = r
            total = total + jnp.sum(r * r, axis=1, keepdims=True)
            gn = gain_ref[:, pl.ds(pl.multiple_of(e * width + cols.start, HD), HD)].astype(jnp.float32)
            gall[e, rowsof(z), cols] = (r * gn).astype(jnp.bfloat16)

    own = gall.at[e, rowsof(z)]
    sends = []
    gz = []
    ssq[0] = jnp.broadcast_to(total, (tok, 128))
    qc = []
    for i, pe in enumerate((ex, ec, ed)):
        cp = remote(ssq.at[0], ssq.at[i + 1], q_s.at[i], q_r.at[i], (y, z, pe))
        cp.start()
        qc.append(cp)
    for d in range(1, nz):
        cp = remote(own, own, gz_s.at[d], gz_r.at[d], (y, up_to(d), e))
        cp.start()
        gz.append(cp)

    def forward(zi, d):
        blk = gall.at[e, rowsof(zi)]
        a = remote(blk, blk, gx_s.at[d], gx_r.at[d], to_x)
        a.start()
        b = remote(blk, blk, gc_s.at[0, d], gc_r.at[0, d], to_c)
        b.start()
        sends.extend([a, b])

    forward(z, 0)
    for cp in qc:
        cp.wait_recv()
    ms = ssq[0] + ssq[1] + ssq[2] + ssq[3]
    scale = lax.rsqrt(ms * (1.0 / (4 * width)) + 1e-05)
    meta[rowsof(z), :] = jnp.where(lane == 4, scale, wts)
    mc = []
    for d in range(1, nz):
        blk = meta.at[rowsof(z)]
        cp = remote(blk, blk, m_s.at[d], m_r.at[d], (y, up_to(d), e))
        cp.start()
        mc.append(cp)
    for d in range(1, nz):
        gz[d - 1].wait_recv()
        forward(down_to(d), d)
    def half(slot, slices):
        acc = jnp.zeros((rows, CW), jnp.float32)
        for i in slices:
            acc = acc + jnp.dot(
                gall[i], wbuf[slot, pl.ds(pl.multiple_of(i * width, width), width), :],
                preferred_element_type=jnp.float32,
            )
        return acc

    for d in range(nz):
        blk = gall.at[ec, rowsof(down_to(d))]
        remote(blk, blk, gc_s.at[0, d], gc_r.at[0, d], to_c).wait_recv()
    for d in range(nz):
        if d < SLOTS // 2:
            gate_copy(d, 2 * d).wait()
            up_copy(d, 2 * d + 1).wait()
            pacc[2 * d] = half(2 * d, (e, ec))
            pacc[2 * d + 1] = half(2 * d + 1, (e, ec))
        zi = down_to(d)
        blk = gall.at[ex, rowsof(zi)]
        remote(blk, blk, gx_s.at[d], gx_r.at[d], to_x).wait_recv()
        b = remote(blk, blk, gc_s.at[1, d], gc_r.at[1, d], to_c)
        b.start()
        sends.append(b)
    for cp in mc:
        cp.wait_recv()
    for d in range(nz):
        zi = down_to(d)
        blk = gall.at[ed, rowsof(zi)]
        remote(blk, blk, gc_s.at[1, d], gc_r.at[1, d], to_c).wait_recv()

    scol = meta[:, 4:5]
    mlane = lax.broadcasted_iota(jnp.int32, (rows, 128), 1)
    wcol = jnp.sum(jnp.where(mlane == e, meta[...], 0.0), axis=1, keepdims=True)

    def pair(j, early):
        sg = lax.rem(2 * j, SLOTS)
        su = lax.rem(2 * j + 1, SLOTS)
        if early:
            gate = (pacc[2 * j] + half(sg, (ex, ed))) * scol
            upv = (pacc[2 * j + 1] + half(su, (ex, ed))) * scol
        else:
            gate_copy(j, sg).wait()
            up_copy(j, su).wait()
            gate = half(sg, (e, ec, ex, ed)) * scol
            upv = half(su, (e, ec, ex, ed)) * scol
        hv = (gate / (1.0 + jnp.exp(-gate))) * upv
        act[:, pl.ds(pl.multiple_of(j * CW, CW), CW)] = hv.astype(jnp.bfloat16)
        nxt = 2 * j + SLOTS

        @pl.when(nxt < 2 * n_pair)
        def _():
            gate_copy(nxt // 2, sg).start()
            up_copy(nxt // 2, su).start()

        @pl.when((nxt >= 2 * n_pair) & (nxt < n_chunks))
        def _():
            for cp in down_copies(nxt - 2 * n_pair, sg) + down_copies(nxt + 1 - 2 * n_pair, su):
                cp.start()

    @pl.loop(0, SLOTS // 2)
    def _(j):
        pair(j, True)

    @pl.loop(SLOTS // 2, n_pair)
    def _(j):
        pair(j, False)

    def down_slice(pos):
        @pl.loop(0, per_slice)
        def _(i):
            k = pos * per_slice + i
            slot = lax.rem(2 * n_pair + k, SLOTS)
            for t, cp in enumerate(down_copies(k, slot)):
                cp.wait()
                o = jnp.dot(
                    act[...], wbuf[slot, t * ffl : (t + 1) * ffl, :],
                    preferred_element_type=jnp.float32,
                )
                col = pl.ds(pl.multiple_of((i * three + t) * CW, CW), CW)
                part[pos, :, col] = (o * wcol).astype(jnp.bfloat16)

    def to_core(pos):
        cp = remote(part.at[pos], rcore.at[pos // 2], pc_s.at[pos // 2], pc_r.at[pos // 2], to_c)
        cp.start()
        return cp

    down_slice(0)
    pc = [to_core(0)]
    down_slice(1)
    pc[0].wait_recv()
    steps = [2, 1, 3, 0] if nz == 4 else list(range(1, nz)) + [0]
    px = []
    for n, d in enumerate(steps):
        rr = rowsof(up_to(d))
        part[1, rr, :] = (
            part[1, rr, :].astype(jnp.float32) + rcore[0, rr, :].astype(jnp.float32)
        ).astype(jnp.bfloat16)
        cp = remote(part.at[1, rr], rx.at[rr], px_s.at[n], px_r.at[n], to_x)
        cp.start()
        px.append(cp)
    down_slice(2)
    pc.append(to_core(2))
    down_slice(3)
    pc[1].wait_recv()
    pz = []
    for n, d in enumerate(steps):
        rr = rowsof(up_to(d))
        px[n].wait_recv()
        sm = (
            part[3, rr, :].astype(jnp.float32)
            + rcore[1, rr, :].astype(jnp.float32)
            + rx[rr, :].astype(jnp.float32)
        )
        if d:
            part[3, rr, :] = sm.astype(jnp.bfloat16)
            cp = remote(part.at[3, rr], rz.at[d - 1], pz_s.at[d], pz_r.at[d], (y, up_to(d), e))
            cp.start()
            pz.append(cp)
        else:
            res[...] = res[...] + sm
    for cp in pz:
        cp.wait_recv()
    fin = res[...]
    for d in range(1, nz):
        fin = fin + rz[d - 1].astype(jnp.float32)
    out_ref[...] = fin.astype(jnp.bfloat16)
    for cp in kv + qc + mc + gz + sends + pc + px + pz:
        cp.wait_send()


def fused(
    hidden_in, queries, keys, values, norm_gain, routes, gate_codes, lengths, w_gate, w_up, w_down
):
    nz = lax.axis_size("attn")
    tok, width = queries.shape
    rows, full, ffl = nz * tok, hidden_in.shape[1], w_gate.shape[2]
    bf, f32, dma = jnp.bfloat16, jnp.float32, pltpu.SemaphoreType.DMA
    vm = pl.BlockSpec(memory_space=pltpu.VMEM)
    hbm = pl.BlockSpec(memory_space=pl.ANY)
    return pl.pallas_call(
        functools.partial(fused_kernel, nz),
        out_shape=jax.ShapeDtypeStruct((tok, width), bf),
        in_specs=[vm] * 6 + [pl.BlockSpec(memory_space=pltpu.SMEM)] + [hbm] * 4,
        out_specs=vm,
        scratch_shapes=[
            pltpu.VMEM((SLOTS, full, CW), bf),
            pltpu.VMEM((rows, keys.shape[1]), bf),
            pltpu.VMEM((rows, keys.shape[1]), bf),
            pltpu.VMEM((tok, width), bf),
            pltpu.VMEM((tok, width), f32),
            pltpu.VMEM((4, rows, width), bf),
            pltpu.VMEM((rows, 128), f32),
            pltpu.VMEM((4, tok, 128), f32),
            pltpu.VMEM((rows, ffl), bf),
            pltpu.VMEM((4, rows, width), bf),
            pltpu.VMEM((2, rows, width), bf),
            pltpu.VMEM((rows, width), bf),
            pltpu.VMEM((nz - 1, tok, width), bf),
            pltpu.VMEM((SLOTS, rows, CW), f32),
            dma((SLOTS, full // ffl)),
            dma,
            dma((2, nz)), dma((2, nz)),
            dma((3,)), dma((3,)),
            dma((nz,)), dma((nz,)),
            dma((nz,)), dma((nz,)),
            dma((nz,)), dma((nz,)),
            dma((2, nz)), dma((2, nz)),
            dma((2,)), dma((2,)),
            dma((nz,)), dma((nz,)),
            dma((nz,)), dma((nz,)),
        ],
        compiler_params=pltpu.CompilerParams(
            collective_id=0, has_side_effects=True, vmem_limit_bytes=62 * 2**20
        ),
    )(
        queries, keys, values, norm_gain.reshape(1, full), routes.T, gate_codes.T, lengths,
        hidden_in, w_gate, w_up, w_down,
    )


def fits(mesh, w_gate):
    nz, ffl = mesh.shape["attn"], w_gate.shape[2] // mesh.shape["attn"]
    return nz == 4 and mesh.shape["expert"] == 4 and 3 * ffl == w_gate.shape[1]


def solution(mesh):
    placed = (
        P(("groups", "attn"), None),
        P(("groups", "attn"), "expert"),
        P(("groups", "attn"), "expert"),
        P(("groups", "attn"), "expert"),
        P(),
        P(("groups", "attn"), None),
        P(("groups", "attn"), None),
        P("groups"),
        P("expert", None, "attn"),
        P("expert", None, "attn"),
        P("expert", "attn", None),
    )

    def run(*args):
        return jax.shard_map(
            fused if fits(mesh, args[8]) else local,
            mesh=mesh,
            in_specs=placed,
            out_specs=P(("groups", "attn"), "expert"),
            check_vma=False,
        )(*args)

    return run
```
